256 devices in a mesh: pts: 16 (over x, y), tm: 16 (over z, core).
Axes of the slice: x: 4, y: 4, z: 8, core: 2. Of those that a mesh axis runs over, the one named last changes fastest.
Arguments:
- snapshots: bfloat16 [1024, 3, 131072], P('tm', None, 'pts'), may hold values from -13 to 13
- tail: bfloat16 [64, 3, 131072], P(None, None, 'pts'), may hold values from -13 to 13
- quad_weights: float32 [3, 131072], P(None, 'pts'), may hold values from 0.1 to 1
Outputs:
- modes: bfloat16 [64, 16, 2, 3, 131072], P('tm', None, None, None, 'pts')
The draws below stay inside these ranges and needn't reach their ends.
All inputs are finite; a program needn't handle non-finite values.
Results may differ from the reference program's by a relative error of at most 0.0065.
Values may be sent and summed in bfloat16 or wider, within the bound.
No kernel may reach another device: no remote copies, remote signals or barrier semaphores. Data moves between devices by JAX's collectives and lax.ppermute only.
A program may use at most 64 MiB of HBM per device.

```python
import math
import jax
import jax.numpy as jnp
from jax import lax

VARS = 3
NFFT = 128
NF = 64
PTS_DEV = 8192
HALF = 64
NB = 16
NT = 1024
POINTS = 131072
N_PTS = 16


def tone_field(key, first, count):
    bins = jax.random.randint(jax.random.fold_in(key, 11), (VARS, POINTS), 0, NF)
    offset = jax.random.uniform(jax.random.fold_in(key, 12), (VARS, POINTS), jnp.float32)
    phase = jax.random.uniform(jax.random.fold_in(key, 13), (VARS, POINTS), jnp.float32, 0.0, 2.0 * math.pi)
    amplitude = jnp.exp(jax.random.uniform(jax.random.fold_in(key, 14), (VARS, POINTS), jnp.float32, 0.0, math.log(3.0)))
    moments = (first + jnp.arange(count, dtype=jnp.int32))[:, None, None]
    whole_turns = (bins[None] * moments % NFFT).astype(jnp.float32) / NFFT
    part_turns = offset[None] * (moments.astype(jnp.float32) / NFFT)
    tone = amplitude[None] * jnp.cos(2.0 * math.pi * (whole_turns + part_turns) + phase[None])
    envelope = 0.6 + 1.2 * jnp.arange(POINTS, dtype=jnp.float32) / POINTS
    return (tone, envelope)


def noise_of(key, count):
    return jnp.clip(jax.random.normal(key, (count, VARS, POINTS), jnp.float32), -4.0, 4.0)


def draw_snapshots(key, part):
    tone, envelope = tone_field(key, 0, NT)
    key = jax.random.fold_in(key, 1)
    return (envelope * (noise_of(key, NT) + tone)).astype(jnp.bfloat16)


def draw_tail(key, part):
    tone, envelope = tone_field(key, NT, HALF)
    key = jax.random.fold_in(key, 2)
    return (envelope * (noise_of(key, HALF) + tone)).astype(jnp.bfloat16)


def level_of(own_key, extent, shards, least, top_value):
    loudness = 1.0
    for axis_at, shards_of in shards:
        draws = jax.random.uniform(jax.random.fold_in(jax.random.fold_in(own_key, 6), axis_at), (shards_of,), jnp.float32, least / len(shards), top_value / len(shards))
        loudness = loudness * jnp.repeat(jnp.exp(draws), extent[axis_at] // shards_of).reshape((-1,) + (1,) * (len(extent) - 1 - axis_at))
    return loudness


def setup_inputs(seed: int = 0) -> dict:
    arg_keys = jax.random.split(jax.random.key(seed), 4)
    return {
        "snapshots": draw_snapshots(jax.random.fold_in(arg_keys[3], 71), 0),
        "tail": draw_tail(jax.random.fold_in(arg_keys[3], 71), 0),
        "quad_weights": jnp.clip(jnp.exp(math.log(1.0) - 2.3025851 * jax.random.uniform(arg_keys[2], (VARS, POINTS), jnp.float32) ** level_of(arg_keys[2], (VARS, POINTS), ((1, 16),), -0.2, 0.2)), 0.1, 1.0),
    }


def window_table(length, freq_count):
    steps = jnp.arange(length, dtype=jnp.int32)
    freqs = jnp.arange(freq_count, dtype=jnp.int32)
    hann = 0.5 - 0.5 * jnp.cos(2.0 * math.pi * steps.astype(jnp.float32) / length)
    scale = 1.0 / jnp.sqrt(jnp.sum(hann * hann))
    phase = steps[:, None] * freqs[None, :] % length
    angle = 2.0 * math.pi * phase.astype(jnp.float32) / length
    real_part = (hann * scale)[:, None] * jnp.cos(angle)
    imag_part = -(hann * scale)[:, None] * jnp.sin(angle)
    return jnp.stack([real_part, imag_part], 2).reshape(length, 2 * freq_count).astype(jnp.bfloat16)

def product(pattern, left, right):
    return jnp.einsum(pattern, left.astype(jnp.float32), right.astype(jnp.float32), precision=lax.Precision.HIGHEST)

def spectra_of(halves, dft_table):
    block_count = halves.shape[0] - 1
    blocks = jnp.concatenate([halves[:-1], halves[1:]], 1)
    spectra = product('tk,btvp->bkvp', dft_table, blocks).astype(jnp.bfloat16)
    return spectra.reshape(block_count, dft_table.shape[1] // 2, 2, blocks.shape[2], blocks.shape[3])

def gram_of(spectra, weights):
    weighted = (spectra.astype(jnp.float32) * weights).astype(jnp.bfloat16)
    spec_real, spec_imag = (spectra[:, :, 0], spectra[:, :, 1])
    wgt_real, wgt_imag = (weighted[:, :, 0], weighted[:, :, 1])
    pattern = 'bfvp,cfvp->fbc'
    gram_real = product(pattern, wgt_real, spec_real) + product(pattern, wgt_imag, spec_imag)
    gram_imag = product(pattern, wgt_real, spec_imag) - product(pattern, wgt_imag, spec_real)
    return (gram_real, gram_imag)

def modes_of(spectra, gram_real, gram_imag, divisor):
    coef_real = (gram_real / divisor).astype(jnp.bfloat16)
    coef_imag = (gram_imag / divisor).astype(jnp.bfloat16)
    spec_real, spec_imag = (spectra[:, :, 0], spectra[:, :, 1])
    pattern = 'bfvp,fbc->fcvp'
    mode_real = product(pattern, spec_real, coef_real) - product(pattern, spec_imag, coef_imag)
    mode_imag = product(pattern, spec_real, coef_imag) + product(pattern, spec_imag, coef_real)
    return jnp.stack([mode_real, mode_imag], 2).astype(jnp.bfloat16)

def reference(snapshots, tail, quad_weights):
    dft_table = window_table(NFFT, NF)
    record = jnp.concatenate([snapshots, tail], 0).reshape(NB + 1, HALF, VARS, N_PTS, PTS_DEV)
    slabs = jnp.moveaxis(record, 3, 0)
    weight_slabs = jnp.moveaxis(quad_weights.reshape(VARS, N_PTS, PTS_DEV), 1, 0)

    def slab_gram(pair):
        return gram_of(spectra_of(pair[0], dft_table), pair[1])
    gram_real, gram_imag = lax.map(slab_gram, (slabs, weight_slabs))
    gram_real = lax.optimization_barrier(jnp.sum(gram_real, 0))
    gram_imag = lax.optimization_barrier(jnp.sum(gram_imag, 0))

    def slab_modes(halves):
        return modes_of(spectra_of(halves, dft_table), gram_real, gram_imag, VARS * POINTS)
    modes = lax.map(slab_modes, slabs)
    modes = jnp.moveaxis(modes, 0, 4)
    return modes.reshape(NF, NB, 2, VARS, POINTS)
```

```python
import math

import jax
import jax.numpy as jnp
import numpy as np
from jax import lax
from jax.experimental import pallas as pl
from jax.experimental.pallas import tpu as pltpu
from jax.sharding import PartitionSpec as P

NF = 64
NFFT = 128
HALF = 64
VARS = 3
NB = 16
OWN = 4
CHIPS = 8
ROWS = 128
CHUNK = 1024
VMEM_LIMIT = 40 * 1024 * 1024


def window_table():
    steps = np.arange(NFFT)
    freqs = np.arange(NF)
    hann = 0.5 - 0.5 * np.cos(2.0 * math.pi * steps / NFFT)
    scale = 1.0 / np.sqrt(np.sum(hann * hann))
    angle = 2.0 * math.pi * (steps[:, None] * freqs[None, :] % NFFT) / NFFT
    real_part = (hann * scale)[:, None] * np.cos(angle)
    imag_part = -(hann * scale)[:, None] * np.sin(angle)
    table = np.stack([real_part, imag_part], 2).reshape(NFFT, 2 * NF).T
    return np.stack([table, np.roll(table, HALF, axis=1)]).astype(jnp.bfloat16)


def row_facts():
    row = np.arange(ROWS)
    chip, odd, freq, part = row // 16, row // 8 % 2, row // 2 % 4, row % 2
    block = np.stack([2 * chip + odd, (2 * chip - odd) % NB])
    return block, freq, part


def gram_selectors():
    block, freq, part = row_facts()
    same = freq[:, None] == freq[None, :]
    real = (same & (part[:, None] == part[None, :])).astype(np.float32)
    sign = np.where(part[:, None] == 0, 1.0, -1.0)
    imag = (same & (part[:, None] != part[None, :])) * sign
    masks = np.stack([real, imag]).astype(np.float32)
    left = (np.arange(NB)[None, :, None] == block[:, None, :]).astype(np.float32)
    col = np.arange(ROWS)
    col_part, col_freq, col_block = col // 64, col // 16 % 4, col % 16
    hit = (block[:, :, None] == col_block) & (freq[None, :, None] == col_freq)
    right = np.stack([hit & (col_part == 0), hit & (col_part == 1)], 1).astype(np.float32)
    return masks, left, right


def mode_selectors():
    block, freq, part = row_facts()
    left = (block[:, :, None] == np.arange(NB)).astype(jnp.bfloat16)
    col = np.arange(ROWS)
    col_part, col_freq, col_block = col // 64, col // 16 % 4, col % 16
    out_freq, out_block, out_part = col // 32, col // 2 % 16, col % 2
    hit = (col_freq[:, None] == out_freq) & (col_block[:, None] == out_block)
    right = np.stack([hit & (col_part[:, None] == 0), hit & (col_part[:, None] == 1)]).astype(jnp.bfloat16)
    same = freq[:, None] == out_freq[None, :]
    real = (same & (part[:, None] == out_part[None, :])).astype(np.float32)
    sign = np.where(out_part[None, :] == 0, -1.0, 1.0)
    imag = (same & (part[:, None] != out_part[None, :])) * sign
    return left, right, np.stack([real, imag]).astype(np.float32)


def dft_kernel(flags, table, own, beside, halo, tail, out):
    tbl = table[0]
    first = jnp.where(flags[1] == 1, tail[0], beside[0])
    second = jnp.where(flags[2] == 1, tail[0], halo[0])
    even = jnp.concatenate([own[0], beside[0]], 0)
    odd = jnp.concatenate([first, second], 0)
    even = jnp.dot(tbl, even, preferred_element_type=jnp.float32)
    odd = jnp.dot(tbl, odd, preferred_element_type=jnp.float32)
    width = even.shape[1]
    both = jnp.concatenate([even.reshape(16, 8, width), odd.reshape(16, 8, width)], 1)
    out[:, 0] = both.astype(jnp.bfloat16)


def dft_call(flags, record, beside, halo, tail):
    table = jnp.asarray(window_table())
    points = record.shape[2]
    part = points // 2
    count = part // CHUNK
    piece = pl.BlockSpec((1, HALF, CHUNK), lambda v, i, flags: (v, 0, i))
    mine = pl.BlockSpec((1, HALF, CHUNK), lambda v, i, flags: (v, 0, flags[0] * count + i))
    return pl.pallas_call(
        dft_kernel,
        grid_spec=pltpu.PrefetchScalarGridSpec(
            num_scalar_prefetch=1,
            grid=(VARS, count),
            in_specs=[
                pl.BlockSpec((1, ROWS, NFFT), lambda v, i, flags: (flags[0], 0, 0)),
                mine,
                piece,
                piece,
                mine,
            ],
            out_specs=pl.BlockSpec((16, 1, 16, CHUNK), lambda v, i, flags: (0, v, 0, i)),
        ),
        out_shape=jax.ShapeDtypeStruct((16, VARS, 16, part), jnp.bfloat16),
        compiler_params=pltpu.CompilerParams(vmem_limit_bytes=VMEM_LIMIT),
        name="dft",
    )(flags, table, record, beside, halo, tail)


def exact_dot(left, right):
    return jnp.dot(left, right, precision=lax.Precision.HIGHEST, preferred_element_type=jnp.float32)


def gram_kernel(spectra, weights, masks, left, right, out, total):
    half, step = pl.program_id(0), pl.program_id(1)

    @pl.when(step == 0)
    def _():
        total[half] = jnp.zeros((ROWS, ROWS), jnp.float32)

    acc = total[half]
    for v in range(VARS):
        spec = spectra[:, 0, v].reshape(ROWS, CHUNK)
        wgt = weights[v : v + 1, :]
        weighted = (spec.astype(jnp.float32) * wgt).astype(jnp.bfloat16)
        acc = acc + lax.dot_general(
            weighted, spec, (((1,), (1,)), ((), ())), preferred_element_type=jnp.float32
        )
    total[half] = acc

    @pl.when((half == 1) & (step == pl.num_programs(1) - 1))
    def _():
        gram = jnp.zeros((NB, ROWS), jnp.float32)
        for k in range(2):
            for part in range(2):
                picked = exact_dot(left[k], total[k] * masks[part])
                gram = gram + exact_dot(picked, right[k, part])
        out[...] = jnp.broadcast_to(gram[None], out.shape)


def gram_call(spectra, weights, copies):
    masks, left, right = gram_selectors()
    part = spectra.shape[-1]
    count = part // CHUNK
    whole = lambda shape: pl.BlockSpec(shape, lambda k, i: (0,) * len(shape))
    return pl.pallas_call(
        gram_kernel,
        grid=(2, count),
        in_specs=[
            pl.BlockSpec((CHIPS, 1, VARS, 16, CHUNK), lambda k, i: (0, k, 0, 0, i)),
            pl.BlockSpec((VARS, CHUNK), lambda k, i: (0, k * count + i)),
            whole(masks.shape),
            whole(left.shape),
            whole(right.shape),
        ],
        out_specs=whole((copies, NB, ROWS)),
        out_shape=jax.ShapeDtypeStruct((copies, NB, ROWS), jnp.float32),
        scratch_shapes=[pltpu.VMEM((2, ROWS, ROWS), jnp.float32)],
        compiler_params=pltpu.CompilerParams(vmem_limit_bytes=VMEM_LIMIT),
        name="gram",
    )(spectra, weights, jnp.asarray(masks), jnp.asarray(left), jnp.asarray(right))


def modes_kernel(divisor, grams, left, right, masks, spectra, out, matrix):
    half, step = pl.program_id(0), pl.program_id(1)

    @pl.when((half == 0) & (step == 0))
    def _():
        coef = (jnp.sum(grams[...], 0) / divisor).astype(jnp.bfloat16)
        for k in range(2):
            rows = jnp.dot(left[k], coef, preferred_element_type=jnp.float32).astype(jnp.bfloat16)
            real = jnp.dot(rows, right[0], preferred_element_type=jnp.float32)
            imag = jnp.dot(rows, right[1], preferred_element_type=jnp.float32)
            full = real * masks[0] + imag * masks[1]
            matrix[k] = full.T.astype(jnp.bfloat16)

    mat = matrix[half]
    for v in range(VARS):
        spec = spectra[:, 0, v].reshape(ROWS, CHUNK)
        modes = jnp.dot(mat, spec, preferred_element_type=jnp.float32).astype(jnp.bfloat16)
        out[:, :, v] = modes.reshape(OWN, NB, 2, CHUNK)


def modes_call(grams, spectra, divisor):
    left, right, masks = mode_selectors()
    part = spectra.shape[-1]
    count = part // CHUNK
    whole = lambda shape: pl.BlockSpec(shape, lambda k, i: (0,) * len(shape))
    return pl.pallas_call(
        lambda *refs: modes_kernel(divisor, *refs),
        grid=(2, count),
        in_specs=[
            whole(grams.shape),
            whole(left.shape),
            whole(right.shape),
            whole(masks.shape),
            pl.BlockSpec((CHIPS, 1, VARS, 16, CHUNK), lambda k, i: (0, k, 0, 0, i)),
        ],
        out_specs=pl.BlockSpec((OWN, NB, VARS, 2, CHUNK), lambda k, i: (0, 0, 0, 0, k * count + i)),
        out_shape=jax.ShapeDtypeStruct((OWN, NB, VARS, 2, 2 * part), jnp.bfloat16),
        scratch_shapes=[pltpu.VMEM((2, ROWS, ROWS), jnp.bfloat16)],
        compiler_params=pltpu.CompilerParams(vmem_limit_bytes=VMEM_LIMIT),
        name="modes",
    )(grams, jnp.asarray(left), jnp.asarray(right), jnp.asarray(masks), spectra)


def shards(snapshots, tail, quad_weights):
    points = snapshots.shape[2]
    part = points // 2
    index = lax.axis_index("tm")
    core, chip = index % 2, index // 2
    record = jnp.transpose(snapshots, (1, 0, 2))
    tail = jnp.transpose(tail, (1, 0, 2))
    own = lax.dynamic_slice_in_dim(record, core * part, part, 2)
    other = lax.dynamic_slice_in_dim(record, (1 - core) * part, part, 2)
    before = [(2 * z + 2, 2 * z) for z in range(CHIPS - 1)]
    after = [((2 * z - 1) % NB, 2 * z + 1) for z in range(CHIPS)]
    halo = lax.ppermute(own, "tm", before + after)
    beside = lax.ppermute(other, "tm", [(i, i ^ 1) for i in range(NB)])
    flags = jnp.stack([core, (index == 1).astype(jnp.int32), (index == NB - 2).astype(jnp.int32)])
    spectra = dft_call(flags, record, beside, halo, tail)
    spectra = lax.all_to_all(spectra, "tm", split_axis=0, concat_axis=0, tiled=True)
    spectra = spectra.reshape(CHIPS, 2, VARS, 16, part)
    slabs = lax.axis_size("pts")
    grams = gram_call(spectra, quad_weights, slabs)
    grams = lax.all_to_all(grams, "pts", split_axis=0, concat_axis=0, tiled=True)
    modes = modes_call(grams, spectra, float(VARS * points * slabs))
    return jnp.transpose(modes, (0, 1, 3, 2, 4))


def solution(mesh):
    placed = (P("tm", None, "pts"), P(None, None, "pts"), P(None, "pts"))
    return jax.shard_map(
        shards,
        mesh=mesh,
        in_specs=placed,
        out_specs=P("tm", None, None, None, "pts"),
        check_vma=False,
    )
```

```python
import math

import jax
import jax.numpy as jnp
import numpy as np
from jax import lax
from jax.experimental import pallas as pl
from jax.experimental.pallas import tpu as pltpu
from jax.sharding import PartitionSpec as P

NF = 64
NFFT = 128
HALF = 64
VARS = 3
NB = 16
OWN = 4
CHIPS = 8
ROWS = 128
CHUNK = 1024
WIDE = 4096
VMEM_LIMIT = 28 * 1024 * 1024
SHIFTS = (4, 3, 5, 2, 6, 1, 7, 0)


def window_tables():
    steps = np.arange(NFFT)
    freqs = np.arange(NF)
    hann = 0.5 - 0.5 * np.cos(2.0 * math.pi * steps / NFFT)
    scale = 1.0 / np.sqrt(np.sum(hann * hann))
    angle = 2.0 * math.pi * (steps[:, None] * freqs[None, :] % NFFT) / NFFT
    real_part = (hann * scale)[:, None] * np.cos(angle)
    imag_part = -(hann * scale)[:, None] * np.sin(angle)
    table = np.stack([real_part, imag_part], 2).reshape(NFFT, 2 * NF).T.astype(jnp.bfloat16)
    rows = table.reshape(CHIPS, 2, 2 * OWN, NFFT).transpose(1, 0, 2, 3)
    shifted = np.stack([rows[i % 2][[(i // 2 + shift) % CHIPS for shift in SHIFTS]] for i in range(NB)])
    swapped = np.stack([rows[0], np.roll(rows[1], HALF, axis=-1)])
    return swapped.reshape(2, ROWS // 2, NFFT), shifted.reshape(NB, ROWS // 2, NFFT)


def iota(shape, axis):
    return lax.broadcasted_iota(jnp.int32, shape, axis)


def row_facts(shape, axis, chip):
    row = iota(shape, axis)
    odd, place = row >> 7, (row >> 4) & 7
    half, freq, part = (row >> 3) & 1, (row >> 1) & 3, row & 1
    shift = sum(jnp.where(place == at, shift, 0) for at, shift in enumerate(SHIFTS))
    source = jnp.where(odd == 1, (chip - shift) & 7, place)
    block = (2 * source + jnp.where(odd == 1, 1 - 2 * half, 0)) & (NB - 1)
    return block, freq, part, half


def dft_even_kernel(flags, table, own_a, own_b, beside_a, beside_b, out):
    def spectrum(first, second):
        both = jnp.concatenate([first[0], second[0]], 0)
        freqs = jnp.dot(table[0], both, preferred_element_type=jnp.float32)
        return freqs.reshape(CHIPS, 2 * OWN, freqs.shape[1])

    both = jnp.concatenate([spectrum(own_a, beside_a), spectrum(own_b, beside_b)], 1)
    out[:, 0] = both.astype(jnp.bfloat16)


def dft_even(flags, record, beside):
    table, _ = window_tables()
    part = record.shape[2] // 2
    count = part // WIDE
    low = pl.BlockSpec((1, HALF, WIDE), lambda v, i, flags: (v, 0, i))
    high = pl.BlockSpec((1, HALF, WIDE), lambda v, i, flags: (v, 0, count + i))
    return pl.pallas_call(
        dft_even_kernel,
        grid_spec=pltpu.PrefetchScalarGridSpec(
            num_scalar_prefetch=1,
            grid=(VARS, count),
            in_specs=[
                pl.BlockSpec((1, ROWS // 2, NFFT), lambda v, i, flags: (flags[0] & 1, 0, 0)),
                low,
                high,
                low,
                high,
            ],
            out_specs=pl.BlockSpec((CHIPS, 1, 16, WIDE), lambda v, i, flags: (0, v, 0, i)),
        ),
        out_shape=jax.ShapeDtypeStruct((CHIPS, VARS, 16, part), jnp.bfloat16),
        compiler_params=pltpu.CompilerParams(vmem_limit_bytes=VMEM_LIMIT),
        name="dft_even",
    )(flags, jnp.asarray(table), record, record, beside, beside)


def dft_odd_kernel(flags, table, own_a, own_b, beside_a, beside_b, halo, swapped, tail_a, tail_b, *outs):
    core, chip = flags[0] & 1, flags[0] >> 1
    pick = lambda cond, yes, no: jnp.where(cond, yes[0], no[0])
    first_a = pick(core == 1, own_a, beside_a)
    second_a = jnp.where(chip == CHIPS - 1, tail_a[0], pick(core == 1, swapped, halo))
    first_b = pick(core == 1, halo, swapped)
    second_b = jnp.where(chip == 0, tail_b[0], pick(core == 1, beside_b, own_b))

    def spectrum(first, second):
        both = jnp.concatenate([first, second], 0)
        freqs = jnp.dot(table[0], both, preferred_element_type=jnp.float32)
        return freqs.reshape(CHIPS, 2 * OWN, freqs.shape[1])

    both = jnp.concatenate([spectrum(first_a, second_a), spectrum(first_b, second_b)], 1)
    both = both.astype(jnp.bfloat16)
    for place, out in enumerate(outs):
        out[0] = both[place]


def dft_odd(flags, record, beside, halo, swapped, tail):
    _, table = window_tables()
    part = record.shape[2] // 2
    count = part // WIDE
    table_spec = pl.BlockSpec((1, ROWS // 2, NFFT), lambda v, i, flags: (flags[0], 0, 0))
    low = pl.BlockSpec((1, HALF, WIDE), lambda v, i, flags: (v, 0, i))
    high = pl.BlockSpec((1, HALF, WIDE), lambda v, i, flags: (v, 0, count + i))
    low_out = pl.BlockSpec((1, 16, WIDE), lambda v, i, flags: (v, 0, i))
    return pl.pallas_call(
        dft_odd_kernel,
        grid_spec=pltpu.PrefetchScalarGridSpec(
            num_scalar_prefetch=1,
            grid=(VARS, count),
            in_specs=[table_spec, low, high, low, high, low, low, low, high],
            out_specs=[low_out] * CHIPS,
        ),
        out_shape=[jax.ShapeDtypeStruct((VARS, 16, part), jnp.bfloat16)] * CHIPS,
        compiler_params=pltpu.CompilerParams(vmem_limit_bytes=VMEM_LIMIT),
        name="dft_odd",
    )(flags, jnp.asarray(table), record, record, beside, beside, halo, swapped, tail, tail)


def exact_dot(left, right):
    return jnp.dot(left, right, precision=lax.Precision.HIGHEST, preferred_element_type=jnp.float32)


def rows_of(pieces, v):
    evens = pieces[0][:, v].reshape(ROWS, pieces[0].shape[-1])
    return jnp.concatenate([evens, *(piece[v] for piece in pieces[1:])], 0)


def gram_kernel(flags, weights_a, weights_b, *refs):
    pieces, out, total = refs[:-2], refs[-2], refs[-1]
    step = pl.program_id(0)

    @pl.when(step == 0)
    def _():
        total[...] = jnp.zeros(total.shape, jnp.float32)

    size = 2 * ROWS
    acc = total[...]
    for v in range(VARS):
        spec = rows_of(pieces, v)
        wgt_a, wgt_b = weights_a[v : v + 1, :], weights_b[v : v + 1, :]
        wgt = jnp.concatenate([jnp.broadcast_to(wgt_a, (8, CHUNK)), jnp.broadcast_to(wgt_b, (8, CHUNK))], 0)
        wide = spec.astype(jnp.float32).reshape(16, 16, CHUNK) * wgt[None]
        weighted = wide.reshape(size, CHUNK).astype(jnp.bfloat16)
        acc = acc + lax.dot_general(
            weighted, spec, (((1,), (1,)), ((), ())), preferred_element_type=jnp.float32
        )
    total[...] = acc

    @pl.when(step == pl.num_programs(0) - 1)
    def _():
        chip = flags[0] >> 1
        _, freq_i, part_i, half_i = row_facts((size, size), 0, chip)
        _, freq_j, part_j, half_j = row_facts((size, size), 1, chip)
        same = (freq_i == freq_j) & (half_i == half_j)
        sums = total[...]
        real = jnp.where(same & (part_i == part_j), sums, 0.0)
        imag = jnp.where(same & (part_i != part_j), jnp.where(part_i == 0, sums, -sums), 0.0)
        block, _, _, _ = row_facts((NB, size), 1, chip)
        left = (iota((NB, size), 0) == block).astype(jnp.float32)
        block, freq, _, _ = row_facts((size, ROWS), 0, chip)
        col = iota((size, ROWS), 1)
        hit = (block == (col & 15)) & (freq == ((col >> 4) & 3))
        right_real = (hit & (col < 64)).astype(jnp.float32)
        right_imag = (hit & (col >= 64)).astype(jnp.float32)
        gram = exact_dot(exact_dot(left, real), right_real) + exact_dot(exact_dot(left, imag), right_imag)
        out[...] = jnp.broadcast_to(gram[None], out.shape)


def piece_specs(variables, points, index):
    even = pl.BlockSpec((CHIPS, variables, 16, points), lambda *at: (0, *index(*at)))
    odd = pl.BlockSpec((variables, 16, points), index)
    return [even] + [odd] * CHIPS


def gram_call(flags, pieces, weights, copies):
    part = pieces[0].shape[-1]
    count = part // CHUNK
    return pl.pallas_call(
        gram_kernel,
        grid_spec=pltpu.PrefetchScalarGridSpec(
            num_scalar_prefetch=1,
            grid=(count,),
            in_specs=[
                pl.BlockSpec((VARS, CHUNK), lambda i, flags: (0, i)),
                pl.BlockSpec((VARS, CHUNK), lambda i, flags: (0, count + i)),
                *piece_specs(VARS, CHUNK, lambda i, flags: (0, 0, i)),
            ],
            out_specs=pl.BlockSpec((copies, NB, ROWS), lambda i, flags: (0, 0, 0)),
            scratch_shapes=[pltpu.VMEM((2 * ROWS, 2 * ROWS), jnp.float32)],
        ),
        out_shape=jax.ShapeDtypeStruct((copies, NB, ROWS), jnp.float32),
        compiler_params=pltpu.CompilerParams(vmem_limit_bytes=VMEM_LIMIT),
        name="gram",
    )(flags, weights, weights, *pieces)


def coefficient_matrix(coef, chip):
    size = 2 * ROWS
    block, _, _, _ = row_facts((size, NB), 0, chip)
    left = (iota((size, NB), 1) == block).astype(jnp.bfloat16)
    rows = jnp.dot(left, coef, preferred_element_type=jnp.float32).astype(jnp.bfloat16)
    col, out = iota((ROWS, size), 0), iota((ROWS, size), 1)
    hit = (col & 63) == ((out >> 1) & 63)
    real = jnp.dot(rows, (hit & (col < 64)).astype(jnp.bfloat16), preferred_element_type=jnp.float32)
    imag = jnp.dot(rows, (hit & (col >= 64)).astype(jnp.bfloat16), preferred_element_type=jnp.float32)
    _, freq, part, half = row_facts((size, size), 0, chip)
    out = iota((size, size), 1)
    same = (freq == ((out >> 5) & 3)) & (half == (out >> 7))
    signed = jnp.where((out & 1) == 0, -imag, imag)
    full = jnp.where(same, jnp.where(part == (out & 1), real, signed), 0.0)
    return full.T.astype(jnp.bfloat16)


def modes_kernel(divisor, flags, grams, *refs):
    pieces, out, matrix = refs[:-2], refs[-2], refs[-1]

    @pl.when(pl.program_id(0) == 0)
    def _():
        coef = (jnp.sum(grams[...], 0) / divisor).astype(jnp.bfloat16)
        matrix[...] = coefficient_matrix(coef, flags[0] >> 1)

    part = pieces[0].shape[-1]
    spec = rows_of(pieces, 0)
    for start in range(0, part, CHUNK):
        modes = jnp.dot(
            matrix[...], spec[:, start : start + CHUNK], preferred_element_type=jnp.float32
        ).astype(jnp.bfloat16)
        for half in range(2):
            at = half * part + start
            rows = modes[half * ROWS : (half + 1) * ROWS]
            out[:, :, 0, :, at : at + CHUNK] = rows.reshape(OWN, NB, 2, CHUNK)


def modes_call(flags, grams, pieces, divisor):
    part = pieces[0].shape[-1]
    return pl.pallas_call(
        lambda *refs: modes_kernel(divisor, *refs),
        grid_spec=pltpu.PrefetchScalarGridSpec(
            num_scalar_prefetch=1,
            grid=(VARS,),
            in_specs=[
                pl.BlockSpec(grams.shape, lambda v, flags: (0, 0, 0)),
                *piece_specs(1, part, lambda v, flags: (v, 0, 0)),
            ],
            out_specs=pl.BlockSpec((OWN, NB, 1, 2, 2 * part), lambda v, flags: (0, 0, v, 0, 0)),
            scratch_shapes=[pltpu.VMEM((2 * ROWS, 2 * ROWS), jnp.bfloat16)],
        ),
        out_shape=jax.ShapeDtypeStruct((OWN, NB, VARS, 2, 2 * part), jnp.bfloat16),
        compiler_params=pltpu.CompilerParams(vmem_limit_bytes=VMEM_LIMIT),
        name="modes",
    )(flags, grams, *pieces)


def shifted_by(value, shift):
    pairs = [(2 * z + k, 2 * ((z + shift) % CHIPS) + k) for z in range(CHIPS) for k in range(2)]
    return lax.ppermute(value, "tm", pairs)


def shards(snapshots, tail, quad_weights):
    points = snapshots.shape[2]
    part = points // 2
    index = lax.axis_index("tm")
    record = jnp.transpose(snapshots, (1, 0, 2))
    tail = jnp.transpose(tail, (1, 0, 2))
    flags = index.astype(jnp.int32)[None]
    across = [(i, i ^ 1) for i in range(NB)]
    own = lax.dynamic_slice_in_dim(record, (index & 1) * part, part, 2)
    before = [(2 * z + 2, 2 * z) for z in range(CHIPS - 1)]
    after = [((2 * z - 1) % NB, 2 * z + 1) for z in range(CHIPS)]
    own, record = lax.optimization_barrier((own, record))
    halo = lax.ppermute(own, "tm", before + after)
    beside = lax.ppermute(record, "tm", across)
    evens = dft_even(flags, record, beside)
    evens, halo = lax.optimization_barrier((evens, halo))
    groups = [list(range(core, NB, 2)) for core in range(2)]
    evens = lax.all_to_all(evens, "tm", split_axis=0, concat_axis=0, axis_index_groups=groups, tiled=True)
    swapped = lax.ppermute(halo, "tm", across)
    odds = dft_odd(flags, record, beside, halo, swapped, tail)
    odds = [shifted_by(odd, shift) if shift else odd for odd, shift in zip(odds, SHIFTS)]
    pieces = [evens, *odds]
    slabs = lax.axis_size("pts")
    grams = gram_call(flags, pieces, quad_weights, slabs)
    grams = lax.all_to_all(grams, "pts", split_axis=0, concat_axis=0, tiled=True)
    modes = modes_call(flags, grams, pieces, float(VARS * points * slabs))
    return jnp.transpose(modes, (0, 1, 3, 2, 4))


def solution(mesh):
    placed = (P("tm", None, "pts"), P(None, None, "pts"), P(None, "pts"))
    return jax.shard_map(
        shards,
        mesh=mesh,
        in_specs=placed,
        out_specs=P("tm", None, None, None, "pts"),
        check_vma=False,
    )
```

```python
import math

import jax
import jax.numpy as jnp
import numpy as np
from jax import lax
from jax.experimental import pallas as pl
from jax.experimental.pallas import tpu as pltpu
from jax.sharding import PartitionSpec as P

NF = 64
NFFT = 128
HALF = 64
VARS = 3
NB = 16
OWN = 4
CHIPS = 8
ROWS = 128
CHUNK = 2048
COVER = 30_000_000_000
HELD = 6
WIDE = 4096
VMEM_LIMIT = 28 * 1024 * 1024
SHIFTS = (4, 3, 5, 2, 6, 1, 7, 0)


def window_tables():
    steps = np.arange(NFFT)
    freqs = np.arange(NF)
    hann = 0.5 - 0.5 * np.cos(2.0 * math.pi * steps / NFFT)
    scale = 1.0 / np.sqrt(np.sum(hann * hann))
    angle = 2.0 * math.pi * (steps[:, None] * freqs[None, :] % NFFT) / NFFT
    real_part = (hann * scale)[:, None] * np.cos(angle)
    imag_part = -(hann * scale)[:, None] * np.sin(angle)
    table = np.stack([real_part, imag_part], 2).reshape(NFFT, 2 * NF).T.astype(jnp.bfloat16)
    rows = table.reshape(CHIPS, 2, 2 * OWN, NFFT).transpose(1, 0, 2, 3)
    shifted = np.stack([rows[i % 2][[(i // 2 + shift) % CHIPS for shift in SHIFTS]] for i in range(NB)])
    swapped = np.stack([rows[0], np.roll(rows[1], HALF, axis=-1)])
    return swapped.reshape(2, ROWS // 2, NFFT), shifted.reshape(NB, ROWS // 2, NFFT)


def iota(shape, axis):
    return lax.broadcasted_iota(jnp.int32, shape, axis)


def row_facts(shape, axis, chip):
    row = iota(shape, axis)
    odd, place = row >> 7, (row >> 4) & 7
    half, freq, part = (row >> 3) & 1, (row >> 1) & 3, row & 1
    shift = sum(jnp.where(place == at, shift, 0) for at, shift in enumerate(SHIFTS))
    source = jnp.where(odd == 1, (chip - shift) & 7, place)
    block = (2 * source + jnp.where(odd == 1, 1 - 2 * half, 0)) & (NB - 1)
    return block, freq, part, half


def dft_even_kernel(flags, table, own_a, own_b, beside_a, beside_b, out):
    def spectrum(first, second):
        both = jnp.concatenate([first[0], second[0]], 0)
        freqs = jnp.dot(table[0], both, preferred_element_type=jnp.float32)
        return freqs.reshape(CHIPS, 2 * OWN, freqs.shape[1])

    both = jnp.concatenate([spectrum(own_a, beside_a), spectrum(own_b, beside_b)], 1)
    out[:, 0] = both.astype(jnp.bfloat16)


def dft_even(flags, record, beside):
    table, _ = window_tables()
    part = record.shape[2] // 2
    count = part // WIDE
    low = pl.BlockSpec((1, HALF, WIDE), lambda v, i, flags: (v, 0, i))
    high = pl.BlockSpec((1, HALF, WIDE), lambda v, i, flags: (v, 0, count + i))
    return pl.pallas_call(
        dft_even_kernel,
        grid_spec=pltpu.PrefetchScalarGridSpec(
            num_scalar_prefetch=1,
            grid=(VARS, count),
            in_specs=[
                pl.BlockSpec((1, ROWS // 2, NFFT), lambda v, i, flags: (flags[0] & 1, 0, 0)),
                low,
                high,
                low,
                high,
            ],
            out_specs=pl.BlockSpec((CHIPS, 1, 16, WIDE), lambda v, i, flags: (0, v, 0, i)),
        ),
        out_shape=jax.ShapeDtypeStruct((CHIPS, VARS, 16, part), jnp.bfloat16),
        compiler_params=pltpu.CompilerParams(vmem_limit_bytes=VMEM_LIMIT),
        name="dft_even",
    )(flags, jnp.asarray(table), record, record, beside, beside)


def dft_odd_kernel(flags, table, own_a, own_b, beside_a, beside_b, halo, swapped, tail_a, tail_b, *outs):
    core, chip = flags[0] & 1, flags[0] >> 1
    pick = lambda cond, yes, no: jnp.where(cond, yes[0], no[0])
    first_a = pick(core == 1, own_a, beside_a)
    second_a = jnp.where(chip == CHIPS - 1, tail_a[0], pick(core == 1, swapped, halo))
    first_b = pick(core == 1, halo, swapped)
    second_b = jnp.where(chip == 0, tail_b[0], pick(core == 1, beside_b, own_b))

    def spectrum(first, second):
        both = jnp.concatenate([first, second], 0)
        freqs = jnp.dot(table[0], both, preferred_element_type=jnp.float32)
        return freqs.reshape(CHIPS, 2 * OWN, freqs.shape[1])

    both = jnp.concatenate([spectrum(first_a, second_a), spectrum(first_b, second_b)], 1)
    both = both.astype(jnp.bfloat16)
    for place, out in enumerate(outs):
        out[0] = both[place]


def dft_odd(flags, record, beside, halo, swapped, tail):
    _, table = window_tables()
    part = record.shape[2] // 2
    count = part // WIDE
    table_spec = pl.BlockSpec((1, ROWS // 2, NFFT), lambda v, i, flags: (flags[0], 0, 0))
    low = pl.BlockSpec((1, HALF, WIDE), lambda v, i, flags: (v, 0, i))
    high = pl.BlockSpec((1, HALF, WIDE), lambda v, i, flags: (v, 0, count + i))
    low_out = pl.BlockSpec((1, 16, WIDE), lambda v, i, flags: (v, 0, i))
    return pl.pallas_call(
        dft_odd_kernel,
        grid_spec=pltpu.PrefetchScalarGridSpec(
            num_scalar_prefetch=1,
            grid=(VARS, count),
            in_specs=[table_spec, low, high, low, high, low, low, low, high],
            out_specs=[low_out] * CHIPS,
        ),
        out_shape=[jax.ShapeDtypeStruct((VARS, 16, part), jnp.bfloat16)] * CHIPS,
        cost_estimate=pl.CostEstimate(flops=COVER, bytes_accessed=COVER, transcendentals=0),
        compiler_params=pltpu.CompilerParams(vmem_limit_bytes=VMEM_LIMIT),
        name="dft_odd",
    )(flags, jnp.asarray(table), record, record, beside, beside, halo, swapped, tail, tail)


def selected(chosen, values, from_left):
    result = None
    for _ in range(3):
        term = values.astype(jnp.bfloat16)
        values = values - term.astype(jnp.float32)
        pair = (chosen, term) if from_left else (term, chosen)
        product = jnp.dot(*pair, preferred_element_type=jnp.float32)
        result = product if result is None else result + product
    return result


def rows_of(pieces, v):
    evens = pieces[0][:, v].reshape(ROWS, pieces[0].shape[-1])
    return jnp.concatenate([evens, *(piece[v] for piece in pieces[1:])], 0)


def held_kernel(evens, weights, evens_out, weights_out):
    evens_out[...] = evens[...]
    weights_out[...] = weights[...]


def held_call(evens, weights):
    part = evens.shape[-1]
    piece = pl.BlockSpec((1, VARS, 16, part), lambda i: (i, 0, 0, 0))
    line = pl.BlockSpec(weights.shape, lambda i: (0, 0))
    return pl.pallas_call(
        held_kernel,
        grid=(CHIPS,),
        in_specs=[piece, line],
        out_specs=[piece, line],
        out_shape=[
            jax.ShapeDtypeStruct(evens.shape, evens.dtype),
            jax.ShapeDtypeStruct(weights.shape, weights.dtype),
        ],
        compiler_params=pltpu.CompilerParams(vmem_limit_bytes=VMEM_LIMIT),
        name="held",
    )(evens, weights)


def gram_kernel(flags, weights_a, weights_b, *refs):
    pieces, out, total = refs[:-2], refs[-2], refs[-1]
    step = pl.program_id(0)

    @pl.when(step == 0)
    def _():
        total[...] = jnp.zeros(total.shape, jnp.float32)

    size = 2 * ROWS
    acc = total[...]
    for v in range(VARS):
        spec = rows_of(pieces, v)
        wgt_a, wgt_b = weights_a[v : v + 1, :], weights_b[v : v + 1, :]
        wgt = jnp.concatenate([jnp.broadcast_to(wgt_a, (8, CHUNK)), jnp.broadcast_to(wgt_b, (8, CHUNK))], 0)
        wide = spec.astype(jnp.float32).reshape(16, 16, CHUNK) * wgt[None]
        weighted = wide.reshape(size, CHUNK).astype(jnp.bfloat16)
        acc = acc + lax.dot_general(
            weighted, spec, (((1,), (1,)), ((), ())), preferred_element_type=jnp.float32
        )
    total[...] = acc

    @pl.when(step == pl.num_programs(0) - 1)
    def _():
        chip = flags[0] >> 1
        sums = total[...]
        mixed = iota((size, size), 0) ^ iota((size, size), 1)
        same = (mixed & 14) == 0
        signed = jnp.where((iota((size, size), 0) & 1) == 0, sums, -sums)
        equal, other = same & ((mixed & 1) == 0), same & ((mixed & 1) == 1)
        masked = jnp.concatenate([jnp.where(equal, sums, 0.0), jnp.where(other, signed, 0.0)], 1)
        block, _, _, _ = row_facts((NB, size), 1, chip)
        left = (iota((NB, size), 0) == block).astype(jnp.bfloat16)
        block, freq, _, _ = row_facts((size, ROWS), 0, chip)
        col = iota((size, ROWS), 1)
        hit = (block == (col & 15)) & (freq == ((col >> 4) & 3))
        right = jnp.concatenate([hit & (col < 64), hit & (col >= 64)], 0).astype(jnp.bfloat16)
        gram = selected(right, selected(left, masked, True), False)
        out[...] = jnp.broadcast_to(gram[None], out.shape)


def piece_specs(variables, points, index):
    even = pl.BlockSpec((CHIPS, variables, 16, points), lambda *at: (0, *index(*at)))
    odd = pl.BlockSpec((variables, 16, points), index)
    return [even] + [odd] * CHIPS


def gram_call(flags, pieces, weights, copies):
    part = pieces[0].shape[-1]
    count = part // CHUNK
    return pl.pallas_call(
        gram_kernel,
        grid_spec=pltpu.PrefetchScalarGridSpec(
            num_scalar_prefetch=1,
            grid=(count,),
            in_specs=[
                pl.BlockSpec((VARS, CHUNK), lambda i, flags: (0, i)),
                pl.BlockSpec((VARS, CHUNK), lambda i, flags: (0, count + i)),
                *piece_specs(VARS, CHUNK, lambda i, flags: (0, 0, i)),
            ],
            out_specs=pl.BlockSpec((copies, NB, ROWS), lambda i, flags: (0, 0, 0)),
            scratch_shapes=[pltpu.VMEM((2 * ROWS, 2 * ROWS), jnp.float32)],
        ),
        out_shape=jax.ShapeDtypeStruct((copies, NB, ROWS), jnp.float32),
        compiler_params=pltpu.CompilerParams(vmem_limit_bytes=VMEM_LIMIT),
        name="gram",
    )(flags, weights, weights, *pieces)


def coefficient_matrix(coef, chip):
    size = 2 * ROWS
    block, _, _, _ = row_facts((size, NB), 0, chip)
    left = (iota((size, NB), 1) == block).astype(jnp.bfloat16)
    rows = jnp.dot(left, coef, preferred_element_type=jnp.float32).astype(jnp.bfloat16)
    col, out = iota((ROWS, size), 0), iota((ROWS, size), 1)
    hit = (col & 63) == ((out >> 1) & 63)
    real = jnp.dot(rows, (hit & (col < 64)).astype(jnp.bfloat16), preferred_element_type=jnp.float32)
    imag = jnp.dot(rows, (hit & (col >= 64)).astype(jnp.bfloat16), preferred_element_type=jnp.float32)
    _, freq, part, half = row_facts((size, size), 0, chip)
    out = iota((size, size), 1)
    same = (freq == ((out >> 5) & 3)) & (half == (out >> 7))
    signed = jnp.where((out & 1) == 0, -imag, imag)
    full = jnp.where(same, jnp.where(part == (out & 1), real, signed), 0.0)
    return full.T.astype(jnp.bfloat16)


def modes_kernel(divisor, flags, grams, *refs):
    pieces, out, matrix = refs[:-2], refs[-2], refs[-1]

    @pl.when(pl.program_id(0) == 0)
    def _():
        coef = (jnp.sum(grams[...], 0) / divisor).astype(jnp.bfloat16)
        matrix[...] = coefficient_matrix(coef, flags[0] >> 1)

    part = pieces[0].shape[-1]
    spec = rows_of(pieces, 0)
    for start in range(0, part, CHUNK):
        modes = jnp.dot(
            matrix[...], spec[:, start : start + CHUNK], preferred_element_type=jnp.float32
        ).astype(jnp.bfloat16)
        for half in range(2):
            at = half * part + start
            rows = modes[half * ROWS : (half + 1) * ROWS]
            out[:, :, 0, :, at : at + CHUNK] = rows.reshape(OWN, NB, 2, CHUNK)


def modes_call(flags, grams, pieces, divisor):
    part = pieces[0].shape[-1]
    return pl.pallas_call(
        lambda *refs: modes_kernel(divisor, *refs),
        grid_spec=pltpu.PrefetchScalarGridSpec(
            num_scalar_prefetch=1,
            grid=(VARS,),
            in_specs=[
                pl.BlockSpec(grams.shape, lambda v, flags: (0, 0, 0)),
                *piece_specs(1, part, lambda v, flags: (v, 0, 0)),
            ],
            out_specs=pl.BlockSpec((OWN, NB, 1, 2, 2 * part), lambda v, flags: (0, 0, v, 0, 0)),
            scratch_shapes=[pltpu.VMEM((2 * ROWS, 2 * ROWS), jnp.bfloat16)],
        ),
        out_shape=jax.ShapeDtypeStruct((OWN, NB, VARS, 2, 2 * part), jnp.bfloat16),
        compiler_params=pltpu.CompilerParams(vmem_limit_bytes=VMEM_LIMIT),
        name="modes",
    )(flags, grams, *pieces)


def shifted_by(value, shift):
    pairs = [(2 * z + k, 2 * ((z + shift) % CHIPS) + k) for z in range(CHIPS) for k in range(2)]
    return lax.ppermute(value, "tm", pairs)


def shards(snapshots, tail, quad_weights):
    points = snapshots.shape[2]
    part = points // 2
    index = lax.axis_index("tm")
    record = jnp.transpose(snapshots, (1, 0, 2))
    tail = jnp.transpose(tail, (1, 0, 2))
    flags = index.astype(jnp.int32)[None]
    across = [(i, i ^ 1) for i in range(NB)]
    own = lax.dynamic_slice_in_dim(record, (index & 1) * part, part, 2)
    before = [(2 * z + 2, 2 * z) for z in range(CHIPS - 1)]
    after = [((2 * z - 1) % NB, 2 * z + 1) for z in range(CHIPS)]
    own, record = lax.optimization_barrier((own, record))
    halo = lax.ppermute(own, "tm", before + after)
    beside = lax.ppermute(record, "tm", across)
    evens = dft_even(flags, record, beside)
    groups = [list(range(core, NB, 2)) for core in range(2)]
    evens = lax.all_to_all(evens, "tm", split_axis=0, concat_axis=0, axis_index_groups=groups, tiled=True)
    swapped = lax.ppermute(halo, "tm", across)
    odds = [*dft_odd(flags, record, beside, halo, swapped, tail)]
    evens, quad_weights = held_call(evens, quad_weights)
    evens, quad_weights, odds[HELD] = lax.optimization_barrier((evens, quad_weights, odds[HELD]))
    odds = [shifted_by(odd, shift) if shift else odd for odd, shift in zip(odds, SHIFTS)]
    pieces = [evens, *odds]
    slabs = lax.axis_size("pts")
    grams = gram_call(flags, pieces, quad_weights, slabs)
    grams = lax.all_to_all(grams, "pts", split_axis=0, concat_axis=0, tiled=True)
    modes = modes_call(flags, grams, pieces, float(VARS * points * slabs))
    return jnp.transpose(modes, (0, 1, 3, 2, 4))


def solution(mesh):
    placed = (P("tm", None, "pts"), P(None, None, "pts"), P(None, "pts"))
    return jax.shard_map(
        shards,
        mesh=mesh,
        in_specs=placed,
        out_specs=P("tm", None, None, None, "pts"),
        check_vma=False,
    )
```

```python
import functools
import math

import jax
import jax.numpy as jnp
import numpy as np
from jax import lax
from jax.experimental import pallas as pl
from jax.experimental.pallas import tpu as pltpu
from jax.sharding import PartitionSpec as P

NF = 64
NFFT = 128
HALF = 64
VARS = 3
NB = 16
OWN = 4
CHIPS = 8
ROWS = 128
CHUNK = 2048
SCALARS = pl.BlockSpec(memory_space=pltpu.SMEM)
NEAR = pl.BlockSpec(memory_space=pltpu.VMEM)
COVER = 30_000_000_000
HELD = 6
WIDE = 4096
VMEM_LIMIT = 28 * 1024 * 1024
SHIFTS = (4, 3, 5, 2, 6, 1, 7, 0)


def window_tables():
    steps = np.arange(NFFT)
    freqs = np.arange(NF)
    hann = 0.5 - 0.5 * np.cos(2.0 * math.pi * steps / NFFT)
    scale = 1.0 / np.sqrt(np.sum(hann * hann))
    angle = 2.0 * math.pi * (steps[:, None] * freqs[None, :] % NFFT) / NFFT
    real_part = (hann * scale)[:, None] * np.cos(angle)
    imag_part = -(hann * scale)[:, None] * np.sin(angle)
    table = np.stack([real_part, imag_part], 2).reshape(NFFT, 2 * NF).T.astype(jnp.bfloat16)
    rows = table.reshape(CHIPS, 2, 2 * OWN, NFFT).transpose(1, 0, 2, 3)
    shifted = np.stack([rows[i % 2][[(i // 2 + shift) % CHIPS for shift in SHIFTS]] for i in range(NB)])
    swapped = np.stack([rows[0], np.roll(rows[1], HALF, axis=-1)])
    return swapped.reshape(2, ROWS // 2, NFFT), shifted.reshape(NB, ROWS // 2, NFFT)


def iota(shape, axis):
    return lax.broadcasted_iota(jnp.int32, shape, axis)


def row_facts(shape, axis, chip):
    row = iota(shape, axis)
    odd, place = row >> 7, (row >> 4) & 7
    half, freq, part = (row >> 3) & 1, (row >> 1) & 3, row & 1
    shift = sum(jnp.where(place == at, shift, 0) for at, shift in enumerate(SHIFTS))
    source = jnp.where(odd == 1, (chip - shift) & 7, place)
    block = (2 * source + jnp.where(odd == 1, 1 - 2 * half, 0)) & (NB - 1)
    return block, freq, part, half


def dft_even_kernel(flags, table, own_a, own_b, beside_a, beside_b, out):
    def spectrum(first, second):
        both = jnp.concatenate([first[0], second[0]], 0)
        freqs = jnp.dot(table[0], both, preferred_element_type=jnp.float32)
        return freqs.reshape(CHIPS, 2 * OWN, freqs.shape[1])

    both = jnp.concatenate([spectrum(own_a, beside_a), spectrum(own_b, beside_b)], 1)
    out[:, 0] = both.astype(jnp.bfloat16)


def dft_even(flags, record, beside):
    table, _ = window_tables()
    part = record.shape[2] // 2
    count = part // WIDE
    low = pl.BlockSpec((1, HALF, WIDE), lambda v, i, flags: (v, 0, i))
    high = pl.BlockSpec((1, HALF, WIDE), lambda v, i, flags: (v, 0, count + i))
    return pl.pallas_call(
        dft_even_kernel,
        grid_spec=pltpu.PrefetchScalarGridSpec(
            num_scalar_prefetch=1,
            grid=(VARS, count),
            in_specs=[
                pl.BlockSpec((1, ROWS // 2, NFFT), lambda v, i, flags: (flags[0] & 1, 0, 0)),
                low,
                high,
                low,
                high,
            ],
            out_specs=pl.BlockSpec((CHIPS, 1, 16, WIDE), lambda v, i, flags: (0, v, 0, i)),
        ),
        out_shape=jax.ShapeDtypeStruct((CHIPS, VARS, 16, part), jnp.bfloat16),
        compiler_params=pltpu.CompilerParams(vmem_limit_bytes=VMEM_LIMIT),
        name="dft_even",
    )(flags, jnp.asarray(table), record, record, beside, beside)


def dft_odd_kernel(flags, table, own_a, own_b, beside_a, beside_b, halo, swapped, tail_a, tail_b, *outs):
    core, chip = flags[0] & 1, flags[0] >> 1
    pick = lambda cond, yes, no: jnp.where(cond, yes[0], no[0])
    first_a = pick(core == 1, own_a, beside_a)
    second_a = jnp.where(chip == CHIPS - 1, tail_a[0], pick(core == 1, swapped, halo))
    first_b = pick(core == 1, halo, swapped)
    second_b = jnp.where(chip == 0, tail_b[0], pick(core == 1, beside_b, own_b))

    def spectrum(first, second):
        both = jnp.concatenate([first, second], 0)
        freqs = jnp.dot(table[0], both, preferred_element_type=jnp.float32)
        return freqs.reshape(CHIPS, 2 * OWN, freqs.shape[1])

    both = jnp.concatenate([spectrum(first_a, second_a), spectrum(first_b, second_b)], 1)
    both = both.astype(jnp.bfloat16)
    for place, out in enumerate(outs):
        out[0] = both[place]


def dft_odd(flags, record, beside, halo, swapped, tail):
    _, table = window_tables()
    part = record.shape[2] // 2
    count = part // WIDE
    table_spec = pl.BlockSpec((1, ROWS // 2, NFFT), lambda v, i, flags: (flags[0], 0, 0))
    low = pl.BlockSpec((1, HALF, WIDE), lambda v, i, flags: (v, 0, i))
    high = pl.BlockSpec((1, HALF, WIDE), lambda v, i, flags: (v, 0, count + i))
    low_out = pl.BlockSpec((1, 16, WIDE), lambda v, i, flags: (v, 0, i))
    return pl.pallas_call(
        dft_odd_kernel,
        grid_spec=pltpu.PrefetchScalarGridSpec(
            num_scalar_prefetch=1,
            grid=(VARS, count),
            in_specs=[table_spec, low, high, low, high, low, low, low, high],
            out_specs=[low_out] * CHIPS,
        ),
        out_shape=[jax.ShapeDtypeStruct((VARS, 16, part), jnp.bfloat16)] * CHIPS,
        cost_estimate=pl.CostEstimate(flops=COVER, bytes_accessed=COVER, transcendentals=0),
        compiler_params=pltpu.CompilerParams(vmem_limit_bytes=VMEM_LIMIT),
        name="dft_odd",
    )(flags, jnp.asarray(table), record, record, beside, beside, halo, swapped, tail, tail)


def selected(chosen, values, from_left):
    result = None
    for _ in range(3):
        term = values.astype(jnp.bfloat16)
        values = values - term.astype(jnp.float32)
        pair = (chosen, term) if from_left else (term, chosen)
        product = jnp.dot(*pair, preferred_element_type=jnp.float32)
        result = product if result is None else result + product
    return result


def rows_of(pieces, v):
    evens = pieces[0][:, v].reshape(ROWS, pieces[0].shape[-1])
    return jnp.concatenate([evens, *(piece[v] for piece in pieces[1:])], 0)


def held_kernel(evens, weights, evens_out, weights_out):
    evens_out[...] = evens[...]
    weights_out[...] = weights[...]


def held_call(evens, weights):
    part = evens.shape[-1]
    piece = pl.BlockSpec((1, VARS, 16, part), lambda i: (i, 0, 0, 0))
    line = pl.BlockSpec(weights.shape, lambda i: (0, 0))
    return pl.pallas_call(
        held_kernel,
        grid=(CHIPS,),
        in_specs=[piece, line],
        out_specs=[piece, line],
        out_shape=[
            jax.ShapeDtypeStruct(evens.shape, evens.dtype),
            jax.ShapeDtypeStruct(weights.shape, weights.dtype),
        ],
        compiler_params=pltpu.CompilerParams(vmem_limit_bytes=VMEM_LIMIT),
        name="held",
    )(evens, weights)


def gram_kernel(flags, weights, *refs):
    pieces, out = refs[:-1], refs[-1]
    part = pieces[0].shape[-1]
    size = 2 * ROWS
    sums = jnp.zeros((size, size), jnp.float32)
    for v in range(VARS):
        for start in range(0, part, CHUNK):
            spec = rows_of([piece.at[..., pl.ds(start, CHUNK)] for piece in pieces], v)
            lines = [weights[v : v + 1, pl.ds(half * part + start, CHUNK)] for half in range(2)]
            wgt = jnp.concatenate([jnp.broadcast_to(line, (8, CHUNK)) for line in lines], 0)
            wide = spec.astype(jnp.float32).reshape(16, 16, CHUNK) * wgt[None]
            weighted = wide.reshape(size, CHUNK).astype(jnp.bfloat16)
            sums = sums + lax.dot_general(
                weighted, spec, (((1,), (1,)), ((), ())), preferred_element_type=jnp.float32
            )
    chip = flags[0] >> 1
    mixed = iota((size, size), 0) ^ iota((size, size), 1)
    same = (mixed & 14) == 0
    signed = jnp.where((iota((size, size), 0) & 1) == 0, sums, -sums)
    equal, other = same & ((mixed & 1) == 0), same & ((mixed & 1) == 1)
    masked = jnp.concatenate([jnp.where(equal, sums, 0.0), jnp.where(other, signed, 0.0)], 1)
    block, _, _, _ = row_facts((NB, size), 1, chip)
    left = (iota((NB, size), 0) == block).astype(jnp.bfloat16)
    block, freq, _, _ = row_facts((size, ROWS), 0, chip)
    col = iota((size, ROWS), 1)
    hit = (block == (col & 15)) & (freq == ((col >> 4) & 3))
    right = jnp.concatenate([hit & (col < 64), hit & (col >= 64)], 0).astype(jnp.bfloat16)
    gram = selected(right, selected(left, masked, True), False)
    out[...] = jnp.broadcast_to(gram[None], out.shape)


def gram_call(flags, pieces, weights, copies):
    return pl.pallas_call(
        gram_kernel,
        in_specs=[SCALARS] + [NEAR] * (1 + len(pieces)),
        out_specs=NEAR,
        out_shape=jax.ShapeDtypeStruct((copies, NB, ROWS), jnp.float32),
        compiler_params=pltpu.CompilerParams(vmem_limit_bytes=VMEM_LIMIT),
        name="gram",
    )(flags, weights, *pieces)


def coefficient_matrix(coef, chip):
    size = 2 * ROWS
    block, _, _, _ = row_facts((size, NB), 0, chip)
    left = (iota((size, NB), 1) == block).astype(jnp.bfloat16)
    rows = jnp.dot(left, coef, preferred_element_type=jnp.float32).astype(jnp.bfloat16)
    col, out = iota((ROWS, size), 0), iota((ROWS, size), 1)
    hit = (col & 63) == ((out >> 1) & 63)
    real = jnp.dot(rows, (hit & (col < 64)).astype(jnp.bfloat16), preferred_element_type=jnp.float32)
    imag = jnp.dot(rows, (hit & (col >= 64)).astype(jnp.bfloat16), preferred_element_type=jnp.float32)
    _, freq, part, half = row_facts((size, size), 0, chip)
    out = iota((size, size), 1)
    same = (freq == ((out >> 5) & 3)) & (half == (out >> 7))
    signed = jnp.where((out & 1) == 0, -imag, imag)
    full = jnp.where(same, jnp.where(part == (out & 1), real, signed), 0.0)
    return full.T.astype(jnp.bfloat16)


def modes_kernel(divisor, flags, grams, *refs):
    pieces, out, held, sems = refs[:-3], *refs[-3:]
    coef = (jnp.sum(grams[...], 0) / divisor).astype(jnp.bfloat16)
    matrix = coefficient_matrix(coef, flags[0] >> 1)
    part = pieces[0].shape[-1]

    def copies(v):
        for freq in range(OWN):
            yield pltpu.make_async_copy(held.at[v, freq], out.at[freq, :, v], sems.at[v, freq])

    for v in range(VARS):
        spec = rows_of(pieces, v)
        for start in range(0, part, CHUNK):
            modes = jnp.dot(
                matrix, spec[:, start : start + CHUNK], preferred_element_type=jnp.float32
            ).astype(jnp.bfloat16)
            for half in range(2):
                at = half * part + start
                rows = modes[half * ROWS : (half + 1) * ROWS]
                held[v, :, :, :, at : at + CHUNK] = rows.reshape(OWN, NB, 2, CHUNK)
        for copy in copies(v):
            copy.start()
    for v in range(VARS):
        for copy in copies(v):
            copy.wait()


def modes_call(flags, grams, pieces, divisor):
    points = 2 * pieces[0].shape[-1]
    return pl.pallas_call(
        functools.partial(modes_kernel, divisor),
        in_specs=[SCALARS] + [NEAR] * (1 + len(pieces)),
        out_specs=pl.BlockSpec(memory_space=pl.ANY),
        scratch_shapes=[
            pltpu.VMEM((VARS, OWN, NB, 2, points), jnp.bfloat16),
            pltpu.SemaphoreType.DMA((VARS, OWN)),
        ],
        out_shape=jax.ShapeDtypeStruct((OWN, NB, VARS, 2, points), jnp.bfloat16),
        compiler_params=pltpu.CompilerParams(vmem_limit_bytes=VMEM_LIMIT),
        name="modes",
    )(flags, grams, *pieces)


def shifted_by(value, shift):
    pairs = [(2 * z + k, 2 * ((z + shift) % CHIPS) + k) for z in range(CHIPS) for k in range(2)]
    return lax.ppermute(value, "tm", pairs)


def shards(snapshots, tail, quad_weights):
    points = snapshots.shape[2]
    part = points // 2
    index = lax.axis_index("tm")
    record = jnp.transpose(snapshots, (1, 0, 2))
    tail = jnp.transpose(tail, (1, 0, 2))
    flags = index.astype(jnp.int32)[None]
    across = [(i, i ^ 1) for i in range(NB)]
    own = lax.dynamic_slice_in_dim(record, (index & 1) * part, part, 2)
    before = [(2 * z + 2, 2 * z) for z in range(CHIPS - 1)]
    after = [((2 * z - 1) % NB, 2 * z + 1) for z in range(CHIPS)]
    halo = lax.ppermute(own, "tm", before + after)
    beside = lax.ppermute(record, "tm", across)
    evens = dft_even(flags, record, beside)
    groups = [list(range(core, NB, 2)) for core in range(2)]
    evens = lax.all_to_all(evens, "tm", split_axis=0, concat_axis=0, axis_index_groups=groups, tiled=True)
    swapped = lax.ppermute(halo, "tm", across)
    odds = [*dft_odd(flags, record, beside, halo, swapped, tail)]
    evens, quad_weights = held_call(evens, quad_weights)
    evens, quad_weights, odds[HELD] = lax.optimization_barrier((evens, quad_weights, odds[HELD]))
    odds = [shifted_by(odd, shift) if shift else odd for odd, shift in zip(odds, SHIFTS)]
    pieces = [evens, *odds]
    slabs = lax.axis_size("pts")
    grams = gram_call(flags, pieces, quad_weights, slabs)
    grams = lax.all_to_all(grams, "pts", split_axis=0, concat_axis=0, tiled=True)
    modes = modes_call(flags, grams, pieces, float(VARS * points * slabs))
    return jnp.transpose(modes, (0, 1, 3, 2, 4))


def solution(mesh):
    placed = (P("tm", None, "pts"), P(None, None, "pts"), P(None, "pts"))
    return jax.shard_map(
        shards,
        mesh=mesh,
        in_specs=placed,
        out_specs=P("tm", None, None, None, "pts"),
        check_vma=False,
    )
```

```python
import functools
import math

import jax
import jax.numpy as jnp
import numpy as np
from jax import lax
from jax.experimental import pallas as pl
from jax.experimental.pallas import tpu as pltpu
from jax.sharding import PartitionSpec as P

NF = 64
NFFT = 128
HALF = 64
VARS = 3
NB = 16
OWN = 4
CHIPS = 8
ROWS = 128
CHUNK = 2048
SCALARS = pl.BlockSpec(memory_space=pltpu.SMEM)
NEAR = pl.BlockSpec(memory_space=pltpu.VMEM)
COVER = 30_000_000_000
HELD = 6
WIDE = 4096
VMEM_LIMIT = 20 * 1024 * 1024
SHIFTS = (4, 3, 5, 2, 6, 1, 7, 0)


def window_tables():
    steps = np.arange(NFFT)
    freqs = np.arange(NF)
    hann = 0.5 - 0.5 * np.cos(2.0 * math.pi * steps / NFFT)
    scale = 1.0 / np.sqrt(np.sum(hann * hann))
    angle = 2.0 * math.pi * (steps[:, None] * freqs[None, :] % NFFT) / NFFT
    real_part = (hann * scale)[:, None] * np.cos(angle)
    imag_part = -(hann * scale)[:, None] * np.sin(angle)
    table = np.stack([real_part, imag_part], 2).reshape(NFFT, 2 * NF).T.astype(jnp.bfloat16)
    rows = table.reshape(CHIPS, 2, 2 * OWN, NFFT).transpose(1, 0, 2, 3)
    shifted = np.stack([rows[i % 2][[(i // 2 + shift) % CHIPS for shift in SHIFTS]] for i in range(NB)])
    swapped = np.stack([rows[0], np.roll(rows[1], HALF, axis=-1)])
    return swapped.reshape(2, ROWS // 2, NFFT), shifted.reshape(NB, ROWS // 2, NFFT)


def iota(shape, axis):
    return lax.broadcasted_iota(jnp.int32, shape, axis)


def row_facts(shape, axis, chip):
    row = iota(shape, axis)
    odd, place = row >> 7, (row >> 4) & 7
    half, freq, part = (row >> 3) & 1, (row >> 1) & 3, row & 1
    shift = sum(jnp.where(place == at, shift, 0) for at, shift in enumerate(SHIFTS))
    source = jnp.where(odd == 1, (chip - shift) & 7, place)
    block = (2 * source + jnp.where(odd == 1, 1 - 2 * half, 0)) & (NB - 1)
    return block, freq, part, half


def dft_even_kernel(flags, table, own_a, own_b, beside_a, beside_b, out):
    def spectrum(first, second):
        both = jnp.concatenate([first[0], second[0]], 0)
        freqs = jnp.dot(table[0], both, preferred_element_type=jnp.float32)
        return freqs.reshape(CHIPS, 2 * OWN, freqs.shape[1])

    both = jnp.concatenate([spectrum(own_a, beside_a), spectrum(own_b, beside_b)], 1)
    out[:, 0] = both.astype(jnp.bfloat16)


def dft_even(flags, record, beside):
    table, _ = window_tables()
    part = record.shape[2] // 2
    count = part // WIDE
    low = pl.BlockSpec((1, HALF, WIDE), lambda v, i, flags: (v, 0, i))
    high = pl.BlockSpec((1, HALF, WIDE), lambda v, i, flags: (v, 0, count + i))
    return pl.pallas_call(
        dft_even_kernel,
        grid_spec=pltpu.PrefetchScalarGridSpec(
            num_scalar_prefetch=1,
            grid=(VARS, count),
            in_specs=[
                pl.BlockSpec((1, ROWS // 2, NFFT), lambda v, i, flags: (flags[0] & 1, 0, 0)),
                low,
                high,
                low,
                high,
            ],
            out_specs=pl.BlockSpec((CHIPS, 1, 16, WIDE), lambda v, i, flags: (0, v, 0, i)),
        ),
        out_shape=jax.ShapeDtypeStruct((CHIPS, VARS, 16, part), jnp.bfloat16),
        compiler_params=pltpu.CompilerParams(vmem_limit_bytes=VMEM_LIMIT),
        name="dft_even",
    )(flags, jnp.asarray(table), record, record, beside, beside)


def dft_odd_kernel(flags, table, own_a, own_b, beside_a, beside_b, halo, swapped, tail_a, tail_b, *outs):
    core, chip = flags[0] & 1, flags[0] >> 1
    pick = lambda cond, yes, no: jnp.where(cond, yes[0], no[0])
    first_a = pick(core == 1, own_a, beside_a)
    second_a = jnp.where(chip == CHIPS - 1, tail_a[0], pick(core == 1, swapped, halo))
    first_b = pick(core == 1, halo, swapped)
    second_b = jnp.where(chip == 0, tail_b[0], pick(core == 1, beside_b, own_b))

    def spectrum(first, second):
        both = jnp.concatenate([first, second], 0)
        freqs = jnp.dot(table[0], both, preferred_element_type=jnp.float32)
        return freqs.reshape(CHIPS, 2 * OWN, freqs.shape[1])

    both = jnp.concatenate([spectrum(first_a, second_a), spectrum(first_b, second_b)], 1)
    both = both.astype(jnp.bfloat16)
    for place, out in enumerate(outs):
        out[0] = both[place]


def dft_odd(flags, record, beside, halo, swapped, tail):
    _, table = window_tables()
    part = record.shape[2] // 2
    count = part // WIDE
    table_spec = pl.BlockSpec((1, ROWS // 2, NFFT), lambda v, i, flags: (flags[0], 0, 0))
    low = pl.BlockSpec((1, HALF, WIDE), lambda v, i, flags: (v, 0, i))
    high = pl.BlockSpec((1, HALF, WIDE), lambda v, i, flags: (v, 0, count + i))
    low_out = pl.BlockSpec((1, 16, WIDE), lambda v, i, flags: (v, 0, i))
    return pl.pallas_call(
        dft_odd_kernel,
        grid_spec=pltpu.PrefetchScalarGridSpec(
            num_scalar_prefetch=1,
            grid=(VARS, count),
            in_specs=[table_spec, low, high, low, high, low, low, low, high],
            out_specs=[low_out] * CHIPS,
        ),
        out_shape=[jax.ShapeDtypeStruct((VARS, 16, part), jnp.bfloat16)] * CHIPS,
        cost_estimate=pl.CostEstimate(flops=COVER, bytes_accessed=COVER, transcendentals=0),
        compiler_params=pltpu.CompilerParams(vmem_limit_bytes=VMEM_LIMIT),
        name="dft_odd",
    )(flags, jnp.asarray(table), record, record, beside, beside, halo, swapped, tail, tail)


def selected(chosen, values, from_left):
    result = None
    for _ in range(3):
        term = values.astype(jnp.bfloat16)
        values = values - term.astype(jnp.float32)
        pair = (chosen, term) if from_left else (term, chosen)
        product = jnp.dot(*pair, preferred_element_type=jnp.float32)
        result = product if result is None else result + product
    return result


def rows_of(pieces, v):
    evens = pieces[0][:, v].reshape(ROWS, pieces[0].shape[-1])
    return jnp.concatenate([evens, *(piece[v] for piece in pieces[1:])], 0)


def held_kernel(flags, evens, weights, evens_out, weights_out, left, right):
    evens_out[...] = evens[...]
    weights_out[...] = weights[...]

    @pl.when(pl.program_id(0) == 0)
    def _():
        chip, size = flags[0] >> 1, 2 * ROWS
        block, _, _, _ = row_facts((NB, size), 1, chip)
        left[...] = (iota((NB, size), 0) == block).astype(jnp.bfloat16)
        block, freq, _, _ = row_facts((size, ROWS), 0, chip)
        col = iota((size, ROWS), 1)
        hit = (block == (col & 15)) & (freq == ((col >> 4) & 3))
        right[...] = jnp.concatenate([hit & (col < 64), hit & (col >= 64)], 0).astype(jnp.bfloat16)


def held_call(flags, evens, weights):
    part = evens.shape[-1]
    piece = pl.BlockSpec((1, VARS, 16, part), lambda i: (i, 0, 0, 0))
    whole = lambda shape: pl.BlockSpec(shape, lambda i: (0, 0))
    left, right = (NB, 2 * ROWS), (4 * ROWS, ROWS)
    return pl.pallas_call(
        held_kernel,
        grid=(CHIPS,),
        in_specs=[SCALARS, piece, whole(weights.shape)],
        out_specs=[piece, whole(weights.shape), whole(left), whole(right)],
        out_shape=[
            jax.ShapeDtypeStruct(evens.shape, evens.dtype),
            jax.ShapeDtypeStruct(weights.shape, weights.dtype),
            jax.ShapeDtypeStruct(left, jnp.bfloat16),
            jax.ShapeDtypeStruct(right, jnp.bfloat16),
        ],
        compiler_params=pltpu.CompilerParams(vmem_limit_bytes=VMEM_LIMIT),
        name="held",
    )(flags, evens, weights)


def gram_kernel(left, right, weights, *refs):
    pieces, out = refs[:-1], refs[-1]
    part = pieces[0].shape[-1]
    size = 2 * ROWS
    sums = jnp.zeros((size, size), jnp.float32)
    for v in range(VARS):
        for start in range(0, part, CHUNK):
            spec = rows_of([piece.at[..., pl.ds(start, CHUNK)] for piece in pieces], v)
            lines = [weights[v : v + 1, pl.ds(half * part + start, CHUNK)] for half in range(2)]
            wgt = jnp.concatenate([jnp.broadcast_to(line, (8, CHUNK)) for line in lines], 0)
            wide = spec.astype(jnp.float32).reshape(16, 16, CHUNK) * wgt[None]
            weighted = wide.reshape(size, CHUNK).astype(jnp.bfloat16)
            sums = sums + lax.dot_general(
                weighted, spec, (((1,), (1,)), ((), ())), preferred_element_type=jnp.float32
            )
    mixed = iota((size, size), 0) ^ iota((size, size), 1)
    same = (mixed & 14) == 0
    signed = jnp.where((iota((size, size), 0) & 1) == 0, sums, -sums)
    equal, other = same & ((mixed & 1) == 0), same & ((mixed & 1) == 1)
    masked = jnp.concatenate([jnp.where(equal, sums, 0.0), jnp.where(other, signed, 0.0)], 1)
    gram = selected(right[...], selected(left[...], masked, True), False)
    out[...] = jnp.broadcast_to(gram[None], out.shape)


def gram_call(selections, pieces, weights, copies):
    return pl.pallas_call(
        gram_kernel,
        in_specs=[NEAR] * (3 + len(pieces)),
        out_specs=NEAR,
        out_shape=jax.ShapeDtypeStruct((copies, NB, ROWS), jnp.float32),
        compiler_params=pltpu.CompilerParams(vmem_limit_bytes=VMEM_LIMIT),
        name="gram",
    )(*selections, weights, *pieces)


def coefficient_matrix(coef, chip):
    size = 2 * ROWS
    block, _, _, _ = row_facts((size, NB), 0, chip)
    left = (iota((size, NB), 1) == block).astype(jnp.bfloat16)
    rows = jnp.dot(left, coef, preferred_element_type=jnp.float32).astype(jnp.bfloat16)
    col, out = iota((ROWS, size), 0), iota((ROWS, size), 1)
    hit = (col & 63) == ((out >> 1) & 63)
    real = jnp.dot(rows, (hit & (col < 64)).astype(jnp.bfloat16), preferred_element_type=jnp.float32)
    imag = jnp.dot(rows, (hit & (col >= 64)).astype(jnp.bfloat16), preferred_element_type=jnp.float32)
    _, freq, part, half = row_facts((size, size), 0, chip)
    out = iota((size, size), 1)
    same = (freq == ((out >> 5) & 3)) & (half == (out >> 7))
    signed = jnp.where((out & 1) == 0, -imag, imag)
    full = jnp.where(same, jnp.where(part == (out & 1), real, signed), 0.0)
    return full.T.astype(jnp.bfloat16)


def modes_kernel(divisor, flags, grams, *refs):
    pieces, out, held, sems = refs[:-3], *refs[-3:]
    coef = (jnp.sum(grams[...], 0) / divisor).astype(jnp.bfloat16)
    matrix = coefficient_matrix(coef, flags[0] >> 1)
    part = pieces[0].shape[-1]

    def copies(v):
        for freq in range(OWN):
            yield pltpu.make_async_copy(held.at[v, freq], out.at[freq, :, v], sems.at[v, freq])

    for v in range(VARS):
        spec = rows_of(pieces, v)
        for start in range(0, part, CHUNK):
            modes = jnp.dot(
                matrix, spec[:, start : start + CHUNK], preferred_element_type=jnp.float32
            ).astype(jnp.bfloat16)
            for half in range(2):
                at = half * part + start
                rows = modes[half * ROWS : (half + 1) * ROWS]
                held[v, :, :, :, at : at + CHUNK] = rows.reshape(OWN, NB, 2, CHUNK)
        for copy in copies(v):
            copy.start()
    for v in range(VARS):
        for copy in copies(v):
            copy.wait()


def modes_call(flags, grams, pieces, divisor):
    points = 2 * pieces[0].shape[-1]
    return pl.pallas_call(
        functools.partial(modes_kernel, divisor),
        in_specs=[SCALARS] + [NEAR] * (1 + len(pieces)),
        out_specs=pl.BlockSpec(memory_space=pl.ANY),
        scratch_shapes=[
            pltpu.VMEM((VARS, OWN, NB, 2, points), jnp.bfloat16),
            pltpu.SemaphoreType.DMA((VARS, OWN)),
        ],
        out_shape=jax.ShapeDtypeStruct((OWN, NB, VARS, 2, points), jnp.bfloat16),
        compiler_params=pltpu.CompilerParams(vmem_limit_bytes=VMEM_LIMIT),
        name="modes",
    )(flags, grams, *pieces)


def shifted_by(value, shift):
    pairs = [(2 * z + k, 2 * ((z + shift) % CHIPS) + k) for z in range(CHIPS) for k in range(2)]
    return lax.ppermute(value, "tm", pairs)


def shards(snapshots, tail, quad_weights):
    points = snapshots.shape[2]
    part = points // 2
    index = lax.axis_index("tm")
    record = jnp.transpose(snapshots, (1, 0, 2))
    tail = jnp.transpose(tail, (1, 0, 2))
    flags = index.astype(jnp.int32)[None]
    across = [(i, i ^ 1) for i in range(NB)]
    own = lax.dynamic_slice_in_dim(record, (index & 1) * part, part, 2)
    before = [(2 * z + 2, 2 * z) for z in range(CHIPS - 1)]
    after = [((2 * z - 1) % NB, 2 * z + 1) for z in range(CHIPS)]
    halo = lax.ppermute(own, "tm", before + after)
    beside = lax.ppermute(record, "tm", across)
    evens = dft_even(flags, record, beside)
    groups = [list(range(core, NB, 2)) for core in range(2)]
    evens = lax.all_to_all(evens, "tm", split_axis=0, concat_axis=0, axis_index_groups=groups, tiled=True)
    swapped = lax.ppermute(halo, "tm", across)
    odds = [*dft_odd(flags, record, beside, halo, swapped, tail)]
    evens, quad_weights, *selections = held_call(flags, evens, quad_weights)
    evens, quad_weights, odds[HELD] = lax.optimization_barrier((evens, quad_weights, odds[HELD]))
    odds = [shifted_by(odd, shift) if shift else odd for odd, shift in zip(odds, SHIFTS)]
    pieces = [evens, *odds]
    slabs = lax.axis_size("pts")
    grams = gram_call(selections, pieces, quad_weights, slabs)
    grams = lax.all_to_all(grams, "pts", split_axis=0, concat_axis=0, tiled=True)
    modes = modes_call(flags, grams, pieces, float(VARS * points * slabs))
    return jnp.transpose(modes, (0, 1, 3, 2, 4))


def solution(mesh):
    placed = (P("tm", None, "pts"), P(None, None, "pts"), P(None, "pts"))
    return jax.shard_map(
        shards,
        mesh=mesh,
        in_specs=placed,
        out_specs=P("tm", None, None, None, "pts"),
        check_vma=False,
    )
```

```python
import functools
import math

import jax
import jax.numpy as jnp
import numpy as np
from jax import lax
from jax.experimental import pallas as pl
from jax.experimental.pallas import tpu as pltpu
from jax.sharding import PartitionSpec as P

NF = 64
NFFT = 128
HALF = 64
VARS = 3
NB = 16
OWN = 4
CHIPS = 8
ROWS = 128
CHUNK = 2048
SCALARS = pl.BlockSpec(memory_space=pltpu.SMEM)
NEAR = pl.BlockSpec(memory_space=pltpu.VMEM)
COVER = 30_000_000_000
HELD = 6
WIDE = 4096
VMEM_LIMIT = 28 * 1024 * 1024
SHIFTS = (2, 6, 3, 5, 4, 1, 7, 0)


def window_tables():
    steps = np.arange(NFFT)
    freqs = np.arange(NF)
    hann = 0.5 - 0.5 * np.cos(2.0 * math.pi * steps / NFFT)
    scale = 1.0 / np.sqrt(np.sum(hann * hann))
    angle = 2.0 * math.pi * (steps[:, None] * freqs[None, :] % NFFT) / NFFT
    real_part = (hann * scale)[:, None] * np.cos(angle)
    imag_part = -(hann * scale)[:, None] * np.sin(angle)
    table = np.stack([real_part, imag_part], 2).reshape(NFFT, 2 * NF).T.astype(jnp.bfloat16)
    rows = table.reshape(CHIPS, 2, 2 * OWN, NFFT).transpose(1, 0, 2, 3)
    shifted = np.stack([rows[i % 2][[(i // 2 + shift) % CHIPS for shift in SHIFTS]] for i in range(NB)])
    swapped = np.stack([rows[0], np.roll(rows[1], HALF, axis=-1)])
    return swapped.reshape(2, ROWS // 2, NFFT), shifted.reshape(NB, ROWS // 2, NFFT)


def iota(shape, axis):
    return lax.broadcasted_iota(jnp.int32, shape, axis)


def row_facts(shape, axis, chip):
    row = iota(shape, axis)
    odd, place = row >> 7, (row >> 4) & 7
    half, freq, part = (row >> 3) & 1, (row >> 1) & 3, row & 1
    shift = sum(jnp.where(place == at, shift, 0) for at, shift in enumerate(SHIFTS))
    source = jnp.where(odd == 1, (chip - shift) & 7, place)
    block = (2 * source + jnp.where(odd == 1, 1 - 2 * half, 0)) & (NB - 1)
    return block, freq, part, half


def dft_even_kernel(flags, table, own_a, own_b, beside_a, beside_b, out):
    def spectrum(first, second):
        both = jnp.concatenate([first[0], second[0]], 0)
        freqs = jnp.dot(table[0], both, preferred_element_type=jnp.float32)
        return freqs.reshape(CHIPS, 2 * OWN, freqs.shape[1])

    both = jnp.concatenate([spectrum(own_a, beside_a), spectrum(own_b, beside_b)], 1)
    out[:, 0] = both.astype(jnp.bfloat16)


def dft_even(flags, record, beside):
    table, _ = window_tables()
    part = record.shape[2] // 2
    count = part // WIDE
    low = pl.BlockSpec((1, HALF, WIDE), lambda v, i, flags: (v, 0, i))
    high = pl.BlockSpec((1, HALF, WIDE), lambda v, i, flags: (v, 0, count + i))
    return pl.pallas_call(
        dft_even_kernel,
        grid_spec=pltpu.PrefetchScalarGridSpec(
            num_scalar_prefetch=1,
            grid=(VARS, count),
            in_specs=[
                pl.BlockSpec((1, ROWS // 2, NFFT), lambda v, i, flags: (flags[0] & 1, 0, 0)),
                low,
                high,
                low,
                high,
            ],
            out_specs=pl.BlockSpec((CHIPS, 1, 16, WIDE), lambda v, i, flags: (0, v, 0, i)),
        ),
        out_shape=jax.ShapeDtypeStruct((CHIPS, VARS, 16, part), jnp.bfloat16),
        compiler_params=pltpu.CompilerParams(vmem_limit_bytes=VMEM_LIMIT),
        name="dft_even",
    )(flags, jnp.asarray(table), record, record, beside, beside)


def dft_odd_kernel(flags, table, own_a, own_b, beside_a, beside_b, halo, swapped, tail_a, tail_b, *outs):
    core, chip = flags[0] & 1, flags[0] >> 1
    pick = lambda cond, yes, no: jnp.where(cond, yes[0], no[0])
    first_a = pick(core == 1, own_a, beside_a)
    second_a = jnp.where(chip == CHIPS - 1, tail_a[0], pick(core == 1, swapped, halo))
    first_b = pick(core == 1, halo, swapped)
    second_b = jnp.where(chip == 0, tail_b[0], pick(core == 1, beside_b, own_b))

    def spectrum(first, second):
        both = jnp.concatenate([first, second], 0)
        freqs = jnp.dot(table[0], both, preferred_element_type=jnp.float32)
        return freqs.reshape(CHIPS, 2 * OWN, freqs.shape[1])

    both = jnp.concatenate([spectrum(first_a, second_a), spectrum(first_b, second_b)], 1)
    both = both.astype(jnp.bfloat16)
    for place, out in enumerate(outs):
        out[0] = both[place]


def dft_odd(flags, record, beside, halo, swapped, tail):
    _, table = window_tables()
    part = record.shape[2] // 2
    count = part // WIDE
    table_spec = pl.BlockSpec((1, ROWS // 2, NFFT), lambda v, i, flags: (flags[0], 0, 0))
    low = pl.BlockSpec((1, HALF, WIDE), lambda v, i, flags: (v, 0, i))
    high = pl.BlockSpec((1, HALF, WIDE), lambda v, i, flags: (v, 0, count + i))
    low_out = pl.BlockSpec((1, 16, WIDE), lambda v, i, flags: (v, 0, i))
    return pl.pallas_call(
        dft_odd_kernel,
        grid_spec=pltpu.PrefetchScalarGridSpec(
            num_scalar_prefetch=1,
            grid=(VARS, count),
            in_specs=[table_spec, low, high, low, high, low, low, low, high],
            out_specs=[low_out] * CHIPS,
        ),
        out_shape=[jax.ShapeDtypeStruct((VARS, 16, part), jnp.bfloat16)] * CHIPS,
        cost_estimate=pl.CostEstimate(flops=COVER, bytes_accessed=COVER, transcendentals=0),
        compiler_params=pltpu.CompilerParams(vmem_limit_bytes=VMEM_LIMIT),
        name="dft_odd",
    )(flags, jnp.asarray(table), record, record, beside, beside, halo, swapped, tail, tail)


def selected(chosen, values, from_left):
    result = None
    for _ in range(3):
        term = values.astype(jnp.bfloat16)
        values = values - term.astype(jnp.float32)
        pair = (chosen, term) if from_left else (term, chosen)
        product = jnp.dot(*pair, preferred_element_type=jnp.float32)
        result = product if result is None else result + product
    return result


def rows_of(pieces, v):
    evens = pieces[0][:, v].reshape(ROWS, pieces[0].shape[-1])
    return jnp.concatenate([evens, *(piece[v] for piece in pieces[1:])], 0)


def held_kernel(evens, weights, evens_out, weights_out):
    evens_out[...] = evens[...]
    weights_out[...] = weights[...]


def held_call(evens, weights):
    part = evens.shape[-1]
    piece = pl.BlockSpec((1, VARS, 16, part), lambda i: (i, 0, 0, 0))
    line = pl.BlockSpec(weights.shape, lambda i: (0, 0))
    return pl.pallas_call(
        held_kernel,
        grid=(CHIPS,),
        in_specs=[piece, line],
        out_specs=[piece, line],
        out_shape=[
            jax.ShapeDtypeStruct(evens.shape, evens.dtype),
            jax.ShapeDtypeStruct(weights.shape, weights.dtype),
        ],
        compiler_params=pltpu.CompilerParams(vmem_limit_bytes=VMEM_LIMIT),
        name="held",
    )(evens, weights)


def gram_kernel(flags, weights, *refs):
    pieces, out = refs[:-1], refs[-1]
    part = pieces[0].shape[-1]
    size = 2 * ROWS
    sums = jnp.zeros((size, size), jnp.float32)
    for v in range(VARS):
        for start in range(0, part, CHUNK):
            spec = rows_of([piece.at[..., pl.ds(start, CHUNK)] for piece in pieces], v)
            lines = [weights[v : v + 1, pl.ds(half * part + start, CHUNK)] for half in range(2)]
            wgt = jnp.concatenate([jnp.broadcast_to(line, (8, CHUNK)) for line in lines], 0)
            wide = spec.astype(jnp.float32).reshape(16, 16, CHUNK) * wgt[None]
            weighted = wide.reshape(size, CHUNK).astype(jnp.bfloat16)
            sums = sums + lax.dot_general(
                weighted, spec, (((1,), (1,)), ((), ())), preferred_element_type=jnp.float32
            )
    chip = flags[0] >> 1
    mixed = iota((size, size), 0) ^ iota((size, size), 1)
    same = (mixed & 14) == 0
    signed = jnp.where((iota((size, size), 0) & 1) == 0, sums, -sums)
    equal, other = same & ((mixed & 1) == 0), same & ((mixed & 1) == 1)
    masked = jnp.concatenate([jnp.where(equal, sums, 0.0), jnp.where(other, signed, 0.0)], 1)
    block, _, _, _ = row_facts((NB, size), 1, chip)
    left = (iota((NB, size), 0) == block).astype(jnp.bfloat16)
    block, freq, _, _ = row_facts((size, ROWS), 0, chip)
    col = iota((size, ROWS), 1)
    hit = (block == (col & 15)) & (freq == ((col >> 4) & 3))
    right = jnp.concatenate([hit & (col < 64), hit & (col >= 64)], 0).astype(jnp.bfloat16)
    gram = selected(right, selected(left, masked, True), False)
    out[...] = jnp.broadcast_to(gram[None], out.shape)


def gram_call(flags, pieces, weights, copies):
    return pl.pallas_call(
        gram_kernel,
        in_specs=[SCALARS] + [NEAR] * (1 + len(pieces)),
        out_specs=NEAR,
        out_shape=jax.ShapeDtypeStruct((copies, NB, ROWS), jnp.float32),
        compiler_params=pltpu.CompilerParams(vmem_limit_bytes=VMEM_LIMIT),
        name="gram",
    )(flags, weights, *pieces)


def coefficient_matrix(coef, chip):
    size = 2 * ROWS
    block, _, _, _ = row_facts((size, NB), 0, chip)
    left = (iota((size, NB), 1) == block).astype(jnp.bfloat16)
    rows = jnp.dot(left, coef, preferred_element_type=jnp.float32).astype(jnp.bfloat16)
    col, out = iota((ROWS, size), 0), iota((ROWS, size), 1)
    hit = (col & 63) == ((out >> 1) & 63)
    real = jnp.dot(rows, (hit & (col < 64)).astype(jnp.bfloat16), preferred_element_type=jnp.float32)
    imag = jnp.dot(rows, (hit & (col >= 64)).astype(jnp.bfloat16), preferred_element_type=jnp.float32)
    _, freq, part, half = row_facts((size, size), 0, chip)
    out = iota((size, size), 1)
    same = (freq == ((out >> 5) & 3)) & (half == (out >> 7))
    signed = jnp.where((out & 1) == 0, -imag, imag)
    full = jnp.where(same, jnp.where(part == (out & 1), real, signed), 0.0)
    return full.T.astype(jnp.bfloat16)


def modes_kernel(divisor, flags, grams, *refs):
    pieces, out, held, sems = refs[:-3], *refs[-3:]
    coef = (jnp.sum(grams[...], 0) / divisor).astype(jnp.bfloat16)
    matrix = coefficient_matrix(coef, flags[0] >> 1)
    part = pieces[0].shape[-1]

    def copies(v):
        for freq in range(OWN):
            yield pltpu.make_async_copy(held.at[v, freq], out.at[freq, :, v], sems.at[v, freq])

    for v in range(VARS):
        spec = rows_of(pieces, v)
        for start in range(0, part, CHUNK):
            modes = jnp.dot(
                matrix, spec[:, start : start + CHUNK], preferred_element_type=jnp.float32
            ).astype(jnp.bfloat16)
            for half in range(2):
                at = half * part + start
                rows = modes[half * ROWS : (half + 1) * ROWS]
                held[v, :, :, :, at : at + CHUNK] = rows.reshape(OWN, NB, 2, CHUNK)
        for copy in copies(v):
            copy.start()
    for v in range(VARS):
        for copy in copies(v):
            copy.wait()


def modes_call(flags, grams, pieces, divisor):
    points = 2 * pieces[0].shape[-1]
    return pl.pallas_call(
        functools.partial(modes_kernel, divisor),
        in_specs=[SCALARS] + [NEAR] * (1 + len(pieces)),
        out_specs=pl.BlockSpec(memory_space=pl.ANY),
        scratch_shapes=[
            pltpu.VMEM((VARS, OWN, NB, 2, points), jnp.bfloat16),
            pltpu.SemaphoreType.DMA((VARS, OWN)),
        ],
        out_shape=jax.ShapeDtypeStruct((OWN, NB, VARS, 2, points), jnp.bfloat16),
        compiler_params=pltpu.CompilerParams(vmem_limit_bytes=VMEM_LIMIT),
        name="modes",
    )(flags, grams, *pieces)


def shifted_by(value, shift):
    pairs = [(2 * z + k, 2 * ((z + shift) % CHIPS) + k) for z in range(CHIPS) for k in range(2)]
    return lax.ppermute(value, "tm", pairs)


def shards(snapshots, tail, quad_weights):
    points = snapshots.shape[2]
    part = points // 2
    index = lax.axis_index("tm")
    record = jnp.transpose(snapshots, (1, 0, 2))
    tail = jnp.transpose(tail, (1, 0, 2))
    flags = index.astype(jnp.int32)[None]
    across = [(i, i ^ 1) for i in range(NB)]
    own = lax.dynamic_slice_in_dim(record, (index & 1) * part, part, 2)
    before = [(2 * z + 2, 2 * z) for z in range(CHIPS - 1)]
    after = [((2 * z - 1) % NB, 2 * z + 1) for z in range(CHIPS)]
    halo = lax.ppermute(own, "tm", before + after)
    beside = lax.ppermute(record, "tm", across)
    evens = dft_even(flags, record, beside)
    groups = [list(range(core, NB, 2)) for core in range(2)]
    evens = lax.all_to_all(evens, "tm", split_axis=0, concat_axis=0, axis_index_groups=groups, tiled=True)
    swapped = lax.ppermute(halo, "tm", across)
    odds = [*dft_odd(flags, record, beside, halo, swapped, tail)]
    evens, quad_weights = held_call(evens, quad_weights)
    evens, quad_weights, odds[HELD] = lax.optimization_barrier((evens, quad_weights, odds[HELD]))
    odds = [shifted_by(odd, shift) if shift else odd for odd, shift in zip(odds, SHIFTS)]
    pieces = [evens, *odds]
    slabs = lax.axis_size("pts")
    grams = gram_call(flags, pieces, quad_weights, slabs)
    grams = lax.all_to_all(grams, "pts", split_axis=0, concat_axis=0, tiled=True)
    modes = modes_call(flags, grams, pieces, float(VARS * points * slabs))
    return jnp.transpose(modes, (0, 1, 3, 2, 4))


def solution(mesh):
    placed = (P("tm", None, "pts"), P(None, None, "pts"), P(None, "pts"))
    return jax.shard_map(
        shards,
        mesh=mesh,
        in_specs=placed,
        out_specs=P("tm", None, None, None, "pts"),
        check_vma=False,
    )
```
